128 devices in a mesh: dp: 4 (over x), tensor: 2 (over core), expert: 16 (over z, y).
Axes of the slice: x: 4, y: 4, z: 4, core: 2. Of those that a mesh axis runs over, the one named last changes fastest.
Arguments:
- tokens: bfloat16 [8192, 2304], P(('dp', 'tensor', 'expert')), may hold values from -6 to 6
- routes: int32 [8192, 2], P(('dp', 'tensor', 'expert')), may hold values from 0 to 7, all different within a row; in each aligned block of 64 rows (0 to 63, 64 to 127, ...) at most 24 rows name the same one
- gates: float32 [8192, 2], P(('dp', 'tensor', 'expert')), may hold values from 0.2 to 1
- segments: int32 [8192], P(('dp', 'tensor', 'expert')), may hold values from 0 to 31, never falling along the last dimension, each value on 1 to 512 neighbouring positions
- w_gate: bfloat16 [16, 2304, 3840], P('expert', None, ('dp', 'tensor')), may hold values from -0.125 to 0.125
- w_up: bfloat16 [16, 2304, 3840], P('expert', None, ('dp', 'tensor')), may hold values from -0.125 to 0.125
- w_down: bfloat16 [16, 3840, 2304], P('expert', ('dp', 'tensor')), may hold values from -0.0625 to 0.0625
Outputs:
- embedded: bfloat16 [8192, 2304], P(('dp', 'tensor', 'expert'))
- pooled: float32 [32, 2304], replicated
The draws below stay inside these ranges and needn't reach their ends.
Inputs may be any that keep to these rules, and one draw needn't show every extreme that they name: `routes`: each residue names two different experts. Within the rows of one device no expert is named more than 24 times, and in every draw some expert is named exactly 24 times by the rows of some device. `segments`: sequence numbers never fall along the residues; each sequence has 1 to 512 residues and one has exactly 512.
All inputs are finite; a program needn't handle non-finite values.
Results may differ from the reference program's by a relative error of at most 0.0085.
Values may be sent and summed in bfloat16 or wider, within the bound.
A program may use at most 64 MiB of HBM per device.

```python
import math
import jax
import jax.numpy as jnp
import numpy as np
from jax import lax

D = 2304
FF = 7680
EXPERTS = 8
TOP = 2
TOK_DEV = 64
SEQ_MAX = 512
CAP = 24
REPL = 2
SLOTS = 16
FF_SLOT = 3840
WSH = 8
FF_DEV = 480
TOKENS = 8192
NSEQ = 32


def levels(rng, dims, shards, smallest, largest):
    gain = 1.0
    for dim, blocks in shards:
        steps = jax.random.uniform(jax.random.fold_in(jax.random.fold_in(rng, 6), dim), (blocks,), jnp.float32, smallest / len(shards), largest / len(shards))
        gain = gain * jnp.repeat(jnp.exp(steps), dims[dim] // blocks).reshape((-1,) + (1,) * (len(dims) - 1 - dim))
    return gain


def length_profile(count, total, bound, lean):
    weights = [(1 << 20) // math.isqrt(rank ** lean) + 1 for rank in range(2, count + 1)]
    surplus, holding = total - bound - (count - 1), [1] * (count - 1)
    while surplus > 0:
        movable = [i for i in range(count - 1) if holding[i] < bound]
        mass, left = sum([weights[i] for i in movable]), surplus
        for i in movable:
            addition = min(bound - holding[i], max(1, left * weights[i] // mass), surplus)
            holding[i] = holding[i] + addition
            surplus = surplus - addition
    return np.array([bound] + holding)


def ragged(own_key, number_of, total, bound, skew):
    if number_of == 2:
        one = jax.random.randint(own_key, (), max(1, total - bound), min(bound, total - 1) + 1)
        return jnp.stack([one, total - one])
    lengths = jnp.asarray(length_profile(number_of, total, bound, skew), jnp.int32)
    pairs = (number_of - 1) // 2
    source_of, taker = lengths[1:1 + 2 * pairs:2], lengths[2:2 + 2 * pairs:2]
    margin = jnp.minimum(source_of - 1, bound - taker)
    passed = jax.random.randint(jax.random.fold_in(own_key, 1), (pairs,), 0, 1 << 20) % (margin + 1)
    lengths = lengths.at[1:1 + 2 * pairs:2].set(source_of - passed).at[2:2 + 2 * pairs:2].set(taker + passed)
    return lengths[jax.random.permutation(jax.random.fold_in(own_key, 2), number_of)]


def deal_out(rng, own, number, rows, count, top, most, slope):
    sequence = jax.random.permutation(rng, count)
    packed, common = portions_of(count, rows * top, most, slope, True), portions_of(count, rows * top, most, slope, False)
    places = jnp.arange(count)

    def named(tallies, turn):
        used = int((tallies > 0).sum())
        fixed = max(1, used // 4)
        moved = fixed + (places - fixed + turn * (used - fixed)) % max(1, count - fixed)
        return jnp.zeros((count,), jnp.int32).at[sequence[jnp.where(places < fixed, places, moved)]].set(jnp.asarray(tallies, jnp.int32))

    tallies = jnp.where(number % 4 == 0, named(packed, number // 4), named(common, number - number // 4 - 1))
    mixed = jax.random.permutation(jax.random.fold_in(own, 3), count)
    giver, receiver = mixed[0:count // 2 * 2:2], mixed[1:count // 2 * 2:2]
    room = jnp.minimum(tallies[giver] - 1, most - tallies[receiver]) // 2
    room = jnp.where((giver == sequence[0]) | (receiver == sequence[0]) | (tallies[receiver] == 0), 0, jnp.maximum(room, 0))
    moved = jax.random.randint(jax.random.fold_in(own, 4), (count // 2,), 0, 1 << 20) % (room + 1)
    tallies = tallies.at[giver].add(-moved).at[receiver].add(moved)
    labels = jnp.searchsorted(jnp.cumsum(tallies), jnp.arange(rows * top), side="right").astype(jnp.int32)
    table = labels.reshape(top, rows).T
    table = table[jax.random.permutation(jax.random.fold_in(own, 1), rows)]
    turn = jax.random.randint(jax.random.fold_in(own, 2), (rows, 1), 0, top)
    return jnp.take_along_axis(table, (jnp.arange(top)[None, :] + turn) % top, axis=1)


def portions_of(count, total, reach, slope, full):
    weights = [(1 << 20) // math.isqrt(rank ** slope) + 1 for rank in range(1, count + 1)]
    largest = reach if full else min(reach, max(-(-total // count), total * weights[0] // sum(weights)))
    least = 1 if total - largest >= count - 1 else 0
    given, spare = [largest] + [least] * (count - 1), total - largest - least * (count - 1)
    while spare > 0:
        movable = [i for i in range(1, count) if given[i] < largest] or [i for i in range(1, count) if given[i] < reach]
        pool, remaining = sum([weights[i] for i in movable]), spare
        for i in movable:
            more = min(reach - given[i], max(1, remaining * weights[i] // pool), spare)
            given[i] = given[i] + more
            spare = spare - more
    return np.array(given)


def gaussian(stream_key, dims, deviation, reach, pieces=(), kind=jnp.bfloat16):
    result = deviation * jax.random.normal(stream_key, dims, jnp.float32)
    if pieces:
        result = result * levels(stream_key, dims, pieces, -0.22, 0.18)
    return jnp.clip(result, -reach, reach).astype(kind)


def setup_inputs(seed: int = 0) -> dict:
    key_list = jax.random.split(jax.random.key(seed), 8)
    tokens = gaussian(key_list[0], (TOKENS, D), 1.0, 6.0, ((0, 128),))
    routes_keys = jax.random.split(jax.random.fold_in(key_list[1], 1), TOKENS // TOK_DEV)
    routes_turns = jax.random.permutation(jax.random.fold_in(key_list[1], 3), TOKENS // TOK_DEV)
    routes = jax.vmap(lambda own, number: deal_out(jax.random.fold_in(key_list[1], 2), own, number, TOK_DEV, EXPERTS, TOP, CAP, 2))(routes_keys, routes_turns).reshape((TOKENS, TOP))
    gates = jnp.clip(0.2 + 0.8 * jax.random.uniform(key_list[2], (TOKENS, TOP), jnp.float32) ** levels(key_list[2], (TOKENS, TOP), ((0, 128),), -0.2, 0.2), 0.2, 1.0)
    segments = jnp.searchsorted(jnp.cumsum(ragged(key_list[3], NSEQ, TOKENS, SEQ_MAX, 2)), jnp.arange(TOKENS), side="right").astype(jnp.int32)
    w_gate = gaussian(key_list[4], (SLOTS, D, FF_SLOT), D ** -0.5, 0.125, ((0, 16), (2, 8)))
    w_up = gaussian(key_list[5], (SLOTS, D, FF_SLOT), D ** -0.5, 0.125, ((0, 16), (2, 8)))
    w_down = gaussian(key_list[6], (SLOTS, FF_SLOT, D), FF ** -0.5, 0.0625, ((0, 16), (1, 8)))
    return {"tokens": tokens, "routes": routes, "gates": gates, "segments": segments, "w_gate": w_gate, "w_up": w_up, "w_down": w_down}


epsilon = 1e-06

def reference(tokens, routes, gates, segments, w_gate, w_up, w_down):
    values = tokens.astype(jnp.float32)
    normed = (values * lax.rsqrt(lax.optimization_barrier(jnp.mean(values * values, axis=1, keepdims=True)) + epsilon)).astype(jnp.bfloat16)
    blocks = TOKENS // TOK_DEV
    flat_routes = routes.reshape(blocks, TOK_DEV * TOP)
    onehot = (flat_routes[:, :, None] == jnp.arange(EXPERTS, dtype=jnp.int32)[None, None, :]).astype(jnp.int32)
    slot_rank = lax.optimization_barrier(jnp.sum((jnp.cumsum(onehot, axis=1) - onehot) * onehot, axis=2))
    block_index = jnp.arange(blocks, dtype=jnp.int32)[:, None]
    slot_index = ((block_index * EXPERTS + flat_routes) * CAP + slot_rank).reshape(-1).astype(jnp.int32)
    source = jnp.repeat(normed, TOP, axis=0)
    buffer = jnp.zeros((blocks * EXPERTS * CAP, D), jnp.bfloat16).at[slot_index].set(source)
    by_expert = buffer.reshape(blocks, EXPERTS, CAP, D).transpose(1, 0, 2, 3).reshape(EXPERTS, blocks * CAP, D)
    gate_full = w_gate.reshape(EXPERTS, REPL, D, FF_SLOT).transpose(0, 2, 1, 3).reshape(EXPERTS, D, FF)
    up_full = w_up.reshape(EXPERTS, REPL, D, FF_SLOT).transpose(0, 2, 1, 3).reshape(EXPERTS, D, FF)
    down_full = w_down.reshape(EXPERTS, FF, D)

    def one_expert(operands):
        row_block, gate_weight, up_weight, down_weight = operands
        gate_proj = jnp.dot(row_block, gate_weight, preferred_element_type=jnp.float32)
        up_proj = jnp.dot(row_block, up_weight, preferred_element_type=jnp.float32)
        hidden = (jax.nn.silu(gate_proj) * up_proj).astype(jnp.bfloat16)
        partials = jnp.einsum('rkf,kfd->krd', hidden.reshape(-1, REPL * WSH, FF_DEV).astype(jnp.float32), down_weight.reshape(REPL * WSH, FF_DEV, D).astype(jnp.float32))
        partials = lax.optimization_barrier(partials.astype(jnp.bfloat16)).astype(jnp.float32)
        group_out = partials.reshape(REPL, WSH, -1, D).sum(axis=1)
        group_out = lax.optimization_barrier(group_out.astype(jnp.bfloat16)).astype(jnp.float32)
        return group_out.sum(axis=0)
    expert_out = lax.map(one_expert, (by_expert, gate_full, up_full, down_full))
    out_flat = expert_out.reshape(EXPERTS, blocks, CAP, D).transpose(1, 0, 2, 3).reshape(-1, D)
    picked = out_flat[slot_index].reshape(TOKENS, TOP, D)
    mixed = values + lax.optimization_barrier(jnp.sum(gates[:, :, None] * picked, axis=1))
    embedded = mixed.astype(jnp.bfloat16)
    seq_hot = (jnp.arange(NSEQ, dtype=jnp.int32)[:, None] == segments[None, :]).astype(jnp.bfloat16)
    seq_sums = jnp.dot(seq_hot, embedded, preferred_element_type=jnp.float32)
    seq_counts = lax.optimization_barrier(jnp.sum(seq_hot.astype(jnp.float32), axis=1))
    pooled = seq_sums / seq_counts[:, None]
    return (embedded, pooled)
```

```python
import jax
import jax.numpy as jnp
from jax import lax
from jax.experimental import pallas as pl
from jax.experimental.pallas import tpu as pltpu
from jax.sharding import PartitionSpec as P

EXPERTS = 8
TOP = 2
CAP = 24
epsilon = 1e-06

NX = 4
NY = 4
NZ = 4
PLANE = NY * NZ
D = 2304
FFD = 480
FFC = 1024
TOK = 64
NSEQ = 32
ROWS = PLANE * CAP
PW = D + 128
MESH = pl.DeviceIdType.MESH
bf16 = jnp.bfloat16
f32 = jnp.float32


def place():
    expert = lax.axis_index("expert")
    return lax.axis_index("dp"), lax.axis_index("tensor"), expert // NY, expert % NY


def moved(dx=0, dc=0, dz=0, dy=0):
    x, c, z, y = place()
    return ((x + dx) % NX, (c + dc) % 2, ((z + dz) % NZ) * NY + (y + dy) % NY)


def dot(a, b, dims=((1,), (0,))):
    return lax.dot_general(a, b, (dims, ((), ())), preferred_element_type=f32)


def kernel(
    tok_ref, routes_ref, gates_ref, seg_ref, wg_ref, wu_ref, wd_ref, emb_ref, pool_ref,
    sbuf, wbuf, rbuf, hbuf, tbuf, vbuf, qbuf, ubuf, ret, pb, pr, p2, p2r, p3,
    w_ls, w_ss, w_rs, d_ss, d_rs, l_s, x_ss, x_rs, y_ss, y_rs, b_ss, b_rs, p_ss, p_rs, p2_ss, p2_rs, p3_ss, p3_rs,
):
    x, c, z, y = place()
    me = lax.axis_index("expert")
    plane = [(dz, dy) for dz in range(NZ) for dy in range(NY) if dz or dy]
    line = [(dx, dc) for dx in range(NX) for dc in range(2) if dx or dc]

    def remote(src, dst, send, recv, target):
        return pltpu.make_async_remote_copy(
            src_ref=src, dst_ref=dst, send_sem=send, recv_sem=recv, device_id=target, device_id_type=MESH
        )

    barrier = pltpu.get_barrier_semaphore()
    for dz, dy in plane:
        pl.semaphore_signal(barrier, inc=1, device_id=moved(0, 0, dz, dy), device_id_type=MESH)
    for dx, dc in line:
        pl.semaphore_signal(barrier, inc=1, device_id=moved(dx, dc), device_id_type=MESH)

    weights = (wg_ref, wu_ref, wd_ref)
    loads = [pltpu.make_async_copy(w, wbuf.at[k, pl.ds(0, FFD)], w_ls.at[k]) for k, w in enumerate(weights)]
    for copy in loads:
        copy.start()

    both = jnp.concatenate(
        [routes_ref[...].astype(f32), gates_ref[...], jnp.zeros((4, TOK), f32)], axis=0
    )
    both = jnp.concatenate([both, jnp.zeros((8, 128 - TOK), f32)], axis=1)
    columns = both.T[:TOK]
    r0, r1 = routes_ref[0:1, :], routes_ref[1:2, :]
    experts = lax.broadcasted_iota(jnp.int32, (EXPERTS, TOK), 0)
    named = jnp.where((experts == r0) | (experts == r1), 1.0, 0.0)
    earlier = lax.broadcasted_iota(jnp.int32, (TOK, TOK), 0) < lax.broadcasted_iota(jnp.int32, (TOK, TOK), 1)
    rank = dot(named.astype(bf16), jnp.where(earlier, 1.0, 0.0).astype(bf16))
    spot = jnp.where(named > 0.5, rank, -1.0)
    slots = lax.broadcasted_iota(jnp.int32, (EXPERTS, CAP, TOK), 1).astype(f32)
    place_rows = jnp.where(slots == spot[:, None, :], 1.0, 0.0).reshape(EXPERTS * CAP, TOK).astype(bf16)

    values = tok_ref[...].astype(f32)
    scale = lax.rsqrt(jnp.mean(values * values, axis=1, keepdims=True) + epsilon)
    normed = (values * scale).astype(bf16)
    sbuf[...] = dot(place_rows, normed).astype(bf16).reshape(EXPERTS, CAP, D)
    wbuf[:, pl.ds(2 * FFD, FFC - 2 * FFD), :] = jnp.zeros((3, FFC - 2 * FFD, D), bf16)

    pl.semaphore_wait(barrier, len(plane) + len(line))

    sends = []
    own = pltpu.make_async_copy(sbuf.at[me // 2], rbuf.at[0, 0], l_s.at[0])
    own.start()
    for dz, dy in plane:
        target = moved(0, 0, dz, dy)
        back = ((NZ - dz) % NZ) * NY + (NY - dy) % NY
        copy = remote(sbuf.at[target[2] // 2], rbuf.at[0, back], d_ss.at[back], d_rs.at[back], target)
        copy.start()
        sends.append(copy)
    pair = [
        remote(w, wbuf.at[k, pl.ds(FFD, FFD)], w_ss.at[k], w_rs.at[k], moved(0, 1))
        for k, w in enumerate(weights)
    ]
    for copy in pair:
        copy.start()

    def group(d, g):
        return rbuf.at[d, pl.ds(g * NY, NY)]

    own.wait()
    for g in range(NZ):
        for i in range(g * NY, (g + 1) * NY):
            if i:
                remote(sbuf.at[0], rbuf.at[0, i], d_ss.at[i], d_rs.at[i], moved()).wait_recv()
        for dx, d in ((1, 3), (3, 1)):
            copy = remote(group(0, g), group(d, g), x_ss.at[d, g], x_rs.at[d, g], moved(dx))
            copy.start()
            sends.append(copy)

    def arrived(d, g):
        remote(group(0, g), group(d, g), x_ss.at[d, g], x_rs.at[d, g], moved(1)).wait_recv()

    def ffn(d):
        @pl.loop(0, FFC // 256)
        def _(j):
            part = pl.ds(pl.multiple_of(j * 256, 256), 256)
            rows = rbuf[d].reshape(ROWS, D)
            gate = dot(rows, wbuf[0, part, :], ((1,), (1,)))
            up = dot(rows, wbuf[1, part, :], ((1,), (1,)))
            hbuf[:, part] = (gate / (1.0 + jnp.exp(-gate)) * up).astype(bf16)

        @pl.loop(0, D // 768)
        def _(j):
            part = pl.ds(pl.multiple_of(j * 768, 256), 768)
            tbuf[d, :, :, part] = dot(hbuf[...], wbuf[2, :, part]).astype(bf16).reshape(PLANE, CAP, 768)

    for copy in loads:
        copy.wait()
    for copy in pair:
        copy.wait()
    ffn(0)
    for k in range(2):
        for d, g, dx in ((3, k, 1), (1, k + 2, 3)):
            arrived(d, g)
            copy = remote(group(d, g), group(2, g), x_ss.at[2, g], x_rs.at[2, g], moved(dx))
            copy.start()
            sends.append(copy)
    for g in (2, 3):
        arrived(3, g)
    ffn(3)

    def half(ref, k):
        return ref.at[pl.ds(k * 8, 8)]

    def give(src, dst, k, dx):
        copy = remote(src, dst, y_ss.at[k], y_rs.at[k], moved(dx))
        copy.start()
        sends.append(copy)

    def taken(dst, k):
        remote(dst, dst, y_ss.at[k], y_rs.at[k], moved(1)).wait_recv()

    give(half(tbuf.at[3], 0), half(vbuf.at[1], 0), 0, 3)
    for g in (0, 1):
        arrived(1, g)
    ffn(1)
    give(half(tbuf.at[1], 1), half(vbuf.at[0], 1), 1, 1)
    for g in range(NZ):
        arrived(2, g)
    ffn(2)
    give(half(tbuf.at[2], 0), qbuf.at[0], 2, 1)
    give(half(tbuf.at[2], 1), qbuf.at[1], 3, 3)

    def add(d, k, q):
        @pl.loop(k * 8, k * 8 + 8)
        def _(i):
            tbuf[d, i] = (tbuf[d, i].astype(f32) + qbuf[q, i - k * 8].astype(f32)).astype(bf16)

    taken(qbuf.at[0], 2)
    add(1, 0, 0)
    give(half(tbuf.at[1], 0), half(vbuf.at[0], 0), 4, 1)
    taken(qbuf.at[1], 3)
    add(3, 1, 1)
    give(half(tbuf.at[3], 1), half(vbuf.at[1], 1), 5, 3)

    taken(half(vbuf.at[1], 0), 0)
    taken(half(vbuf.at[0], 1), 1)
    for k in range(2):
        if k == 0:
            taken(half(vbuf.at[0], 0), 4)
        else:
            taken(half(vbuf.at[1], 1), 5)

        @pl.loop(k * 8, k * 8 + 8)
        def _(i):
            ubuf[i] = (tbuf[0, i].astype(f32) + vbuf[0, i].astype(f32) + vbuf[1, i].astype(f32)).astype(bf16)

        for i in range(k * 8, k * 8 + 8):
            if i:
                target = moved(0, 0, i // NY, i % NY)
                copy = remote(ubuf.at[i], ret.at[me], b_ss.at[i], b_rs.at[me], target)
                copy.start()
                sends.append(copy)
    ret[me] = ubuf[0]

    lanes = lax.broadcasted_iota(jnp.int32, (TOK, 2 * EXPERTS * CAP), 1).astype(f32)
    eights = lax.broadcasted_iota(jnp.int32, (TOK, EXPERTS), 1).astype(f32)
    later = lax.broadcasted_iota(jnp.int32, (TOK, TOK), 0) > lax.broadcasted_iota(jnp.int32, (TOK, TOK), 1)
    q0, q1 = columns[:, 0:1], columns[:, 1:2]
    names = jnp.where((eights == q0) | (eights == q1), 1.0, 0.0)
    ranks = dot(jnp.where(later, 1.0, 0.0).astype(bf16), names.astype(bf16))
    mix = jnp.zeros((TOK, 2 * EXPERTS * CAP), f32)
    for q, gate in ((q0, columns[:, 2:3]), (q1, columns[:, 3:4])):
        at = q * (2 * CAP) + jnp.sum(jnp.where(eights == q, ranks, 0.0), axis=1, keepdims=True)
        mix = mix + jnp.where((lanes == at) | (lanes == at + CAP), gate, 0.0)
    high = mix.astype(bf16)
    low = (mix - high.astype(f32)).astype(bf16)

    for dz, dy in plane:
        target = moved(0, 0, dz, dy)
        remote(ubuf.at[0], ret.at[target[2]], b_ss.at[0], b_rs.at[target[2]], target).wait_recv()
    hot = (lax.broadcasted_iota(jnp.int32, (NSEQ, TOK), 0) == seg_ref[...]).astype(f32)
    count = jnp.broadcast_to(jnp.sum(hot, axis=1, keepdims=True), (NSEQ, 128))
    hot = hot.astype(bf16)

    @pl.loop(0, D // 768)
    def _(j):
        part = pl.ds(pl.multiple_of(j * 768, 256), 768)
        rows = ret[:, :, part].reshape(ROWS, 768)
        mixed = tok_ref[:, part].astype(f32) + (dot(high, rows) + dot(low, rows))
        embedded = mixed.astype(bf16)
        emb_ref[:, part] = embedded
        sums = dot(hot, embedded)
        for i in range(PLANE):
            pb[i, :, part] = sums[2 * i : 2 * i + 2]

    for i in range(PLANE):
        pb[i, :, D:] = count[2 * i : 2 * i + 2]

    for dz, dy in plane:
        target = moved(0, 0, dz, dy)
        copy = remote(pb.at[target[2]], pr.at[me], p_ss.at[target[2]], p_rs.at[me], target)
        copy.start()
        sends.append(copy)
    pr[me] = pb[me]
    for dz, dy in plane:
        target = moved(0, 0, dz, dy)
        remote(pb.at[0], pr.at[target[2]], p_ss.at[0], p_rs.at[target[2]], target).wait_recv()
    p2[...] = jnp.sum(pr[...], axis=0)
    mine = x * 2 + c
    for k, (dx, dc) in enumerate(line):
        target = moved(dx, dc)
        copy = remote(p2, p2r.at[mine], p2_ss.at[k], p2_rs.at[mine], target)
        copy.start()
        sends.append(copy)
    p2r[mine] = p2[...]
    for k, (dx, dc) in enumerate(line):
        target = moved(dx, dc)
        other = target[0] * 2 + target[1]
        remote(p2, p2r.at[other], p2_ss.at[k], p2_rs.at[other], target).wait_recv()
    total = jnp.sum(p2r[...], axis=0)
    p3[me] = total[:, :D] / jnp.concatenate([total[:, D:]] * (D // 128), axis=1)
    for dz, dy in plane:
        target = moved(0, 0, dz, dy)
        copy = remote(p3.at[me], p3.at[me], p3_ss.at[target[2]], p3_rs.at[me], target)
        copy.start()
        sends.append(copy)
    for dz, dy in plane:
        target = moved(0, 0, dz, dy)
        remote(p3.at[target[2]], p3.at[target[2]], p3_ss.at[0], p3_rs.at[target[2]], target).wait_recv()
    for i in range(PLANE):
        pool_ref[2 * i : 2 * i + 2, :] = p3[i]
    for copy in sends:
        copy.wait_send()


def shards(tokens, routes, gates, segments, w_gate, w_up, w_down):
    vmem = pl.BlockSpec(memory_space=pltpu.VMEM)
    hbm = pl.BlockSpec(memory_space=pl.ANY)
    sem = pltpu.SemaphoreType.DMA
    return pl.pallas_call(
        kernel,
        name="moe",
        out_shape=(
            jax.ShapeDtypeStruct((TOK, D), bf16),
            jax.ShapeDtypeStruct((NSEQ, D), f32),
        ),
        in_specs=[vmem] * 4 + [hbm] * 3,
        out_specs=(vmem, vmem),
        scratch_shapes=[
            pltpu.VMEM((EXPERTS, CAP, D), bf16),
            pltpu.VMEM((3, FFC, D), bf16),
            pltpu.VMEM((NX, PLANE, CAP, D), bf16),
            pltpu.VMEM((ROWS, FFC), bf16),
            pltpu.VMEM((NX, PLANE, CAP, D), bf16),
            pltpu.VMEM((2, PLANE, CAP, D), bf16),
            pltpu.VMEM((2, PLANE // 2, CAP, D), bf16),
            pltpu.VMEM((PLANE, CAP, D), bf16),
            pltpu.VMEM((PLANE, CAP, D), bf16),
            pltpu.VMEM((PLANE, 2, PW), f32),
            pltpu.VMEM((PLANE, 2, PW), f32),
            pltpu.VMEM((2, PW), f32),
            pltpu.VMEM((8, 2, PW), f32),
            pltpu.VMEM((PLANE, 2, D), f32),
            sem((3,)), sem((3,)), sem((3,)),
            sem((PLANE,)), sem((PLANE,)), sem((1,)),
            sem((NX, NZ)), sem((NX, NZ)),
            sem((6,)), sem((6,)),
            sem((PLANE,)), sem((PLANE,)),
            sem((PLANE,)), sem((PLANE,)),
            sem((8,)), sem((8,)),
            sem((PLANE,)), sem((PLANE,)),
        ],
        compiler_params=pltpu.CompilerParams(
            collective_id=0, has_side_effects=True, vmem_limit_bytes=58 * 2**20
        ),
    )(
        tokens,
        routes.T,
        gates.T,
        segments[None, :],
        jnp.swapaxes(w_gate[0], 0, 1),
        jnp.swapaxes(w_up[0], 0, 1),
        w_down[0],
    )


def solution(mesh):
    placed = (
        P(("dp", "tensor", "expert"), None),
        P(("dp", "tensor", "expert"), None),
        P(("dp", "tensor", "expert"), None),
        P(("dp", "tensor", "expert")),
        P("expert", None, ("dp", "tensor")),
        P("expert", None, ("dp", "tensor")),
        P("expert", ("dp", "tensor"), None),
    )
    return jax.shard_map(
        shards,
        mesh=mesh,
        in_specs=placed,
        out_specs=(P(("dp", "tensor", "expert"), None), P()),
        check_vma=False,
    )
```

```python
import jax
import jax.numpy as jnp
from jax import lax
from jax.experimental import pallas as pl
from jax.experimental.pallas import tpu as pltpu
from jax.sharding import PartitionSpec as P

EXPERTS = 8
TOP = 2
CAP = 24
epsilon = 1e-06

NX = 4
NY = 4
NZ = 4
PLANE = NY * NZ
D = 2304
FFD = 480
FFC = 1024
TOK = 64
NSEQ = 32
ROWS = PLANE * CAP
CB = 768
CA = D - CB
PW = D + 128
MESH = pl.DeviceIdType.MESH
bf16 = jnp.bfloat16
f32 = jnp.float32


def place():
    expert = lax.axis_index("expert")
    return lax.axis_index("dp"), lax.axis_index("tensor"), expert // NY, expert % NY


def moved(dx=0, dc=0, dz=0, dy=0):
    x, c, z, y = place()
    return ((x + dx) % NX, (c + dc) % 2, ((z + dz) % NZ) * NY + (y + dy) % NY)


def dot(a, b, dims=((1,), (0,))):
    return lax.dot_general(a, b, (dims, ((), ())), preferred_element_type=f32)


def kernel(
    tok_ref, routes_ref, gates_ref, seg_ref, wg_ref, wu_ref, wd_ref, emb_ref, pool_ref,
    sa, sb, wbuf, ra, rb, hbuf, ta, tb, va, qa, ua, reta, retb, raw, meta, mixed, pb, pr, p2, p2r, p3,
    w_ls, w_ss, w_rs, l_s, raw_ss, raw_rs, meta_ss, meta_rs, da_ss, da_rs, db_ss, db_rs, x_ss, x_rs, x2_ss, x2_rs,
    y_ss, y_rs, ba_ss, ba_rs, bb_ss, bb_rs, m_ss, m_rs, p_ss, p_rs, p2_ss, p2_rs, p3_ss, p3_rs,
):
    x, c, z, y = place()
    me = lax.axis_index("expert")
    plane = [(dz, dy) for dz in (0, 3, 2, 1) for dy in range(NY) if dz or dy]
    line = [(dx, dc) for dx in range(NX) for dc in range(2) if dx or dc]
    around = (1, 3, 2)
    sends = []

    def remote(src, dst, send, recv, target):
        return pltpu.make_async_remote_copy(
            src_ref=src, dst_ref=dst, send_sem=send, recv_sem=recv, device_id=target, device_id_type=MESH
        )

    def give(src, dst, send, recv, target):
        copy = remote(src, dst, send, recv, target)
        copy.start()
        sends.append(copy)

    def taken(dst, recv):
        remote(dst, dst, recv, recv, moved(1)).wait_recv()

    barrier = pltpu.get_barrier_semaphore()
    for dz, dy in plane:
        pl.semaphore_signal(barrier, inc=1, device_id=moved(0, 0, dz, dy), device_id_type=MESH)
    for dx, dc in line:
        pl.semaphore_signal(barrier, inc=1, device_id=moved(dx, dc), device_id_type=MESH)

    weights = (wg_ref, wu_ref, wd_ref)
    loads = [pltpu.make_async_copy(w, wbuf.at[k, pl.ds(0, FFD)], w_ls.at[k]) for k, w in enumerate(weights)]
    for copy in loads:
        copy.start()

    meta[0] = jnp.concatenate(
        [
            jnp.concatenate([routes_ref[...].astype(f32), gates_ref[...], jnp.zeros((4, TOK), f32)], axis=0),
            jnp.zeros((8, 128 - TOK), f32),
        ],
        axis=1,
    )
    experts = lax.broadcasted_iota(jnp.int32, (EXPERTS, TOK), 0).astype(f32)
    earlier = lax.broadcasted_iota(jnp.int32, (TOK, TOK), 0) < lax.broadcasted_iota(jnp.int32, (TOK, TOK), 1)
    earlier = jnp.where(earlier, 1.0, 0.0).astype(bf16)
    slots = lax.broadcasted_iota(jnp.int32, (EXPERTS, CAP, TOK), 1).astype(f32)

    def place_rows(d):
        rows = meta[d]
        named = jnp.where((experts == rows[0:1, :TOK]) | (experts == rows[1:2, :TOK]), 1.0, 0.0)
        spot = jnp.where(named > 0.5, dot(named.astype(bf16), earlier), -1.0)
        return jnp.where(slots == spot[:, None, :], 1.0, 0.0).reshape(EXPERTS * CAP, TOK).astype(bf16)

    values = tok_ref[...].astype(f32)
    scale = lax.rsqrt(jnp.mean(values * values, axis=1, keepdims=True) + epsilon)
    normed = (values * scale).astype(bf16)
    raw[0] = normed[:, CA:]

    pl.semaphore_wait(barrier, len(plane) + len(line))
    for dx in around:
        d = (NX - dx) % NX
        give(meta.at[0], meta.at[d], meta_ss.at[d], meta_rs.at[d], moved(dx))
        give(raw.at[0], raw.at[d], raw_ss.at[d], raw_rs.at[d], moved(dx))
    spots = place_rows(0)
    sa[...] = dot(spots, normed[:, :CA]).astype(bf16).reshape(EXPERTS, CAP, CA)
    own = [pltpu.make_async_copy(sa.at[me // 2], ra.at[0, 0], l_s.at[0])]
    own[0].start()
    for dz, dy in plane:
        target = moved(0, 0, dz, dy)
        back = ((NZ - dz) % NZ) * NY + (NY - dy) % NY
        give(sa.at[target[2] // 2], ra.at[back, 0], da_ss.at[back], da_rs.at[back], target)
    for k, w in enumerate(weights):
        give(w, wbuf.at[k, pl.ds(FFD, FFD)], w_ss.at[k], w_rs.at[k], moved(0, 1))
    sb[:, 0] = dot(spots, raw[0]).astype(bf16).reshape(EXPERTS, CAP, CB)
    for d in around:
        taken(meta.at[d], meta_rs.at[d])
        taken(raw.at[d], raw_rs.at[d])
        sb[:, d] = dot(place_rows(d), raw[d]).astype(bf16).reshape(EXPERTS, CAP, CB)
    own.append(pltpu.make_async_copy(sb.at[me // 2], rb.at[0], l_s.at[1]))
    own[1].start()
    for dz, dy in plane:
        target = moved(0, 0, dz, dy)
        back = ((NZ - dz) % NZ) * NY + (NY - dy) % NY
        give(sb.at[target[2] // 2], rb.at[back], db_ss.at[back], db_rs.at[back], target)
    wbuf[:, pl.ds(2 * FFD, FFC - 2 * FFD), :] = jnp.zeros((3, FFC - 2 * FFD, D), bf16)

    def four(g):
        return pl.ds(g * NY, NY)

    def two(g, k):
        return pl.ds(g * NY + 2 * k, 2)

    def forward(g):
        for i in range(g * NY, (g + 1) * NY):
            if i:
                taken(ra.at[i, 0], da_rs.at[i])
            else:
                own[0].wait()
        for dx, d in ((1, 3), (3, 1)):
            give(ra.at[four(g), 0], ra.at[four(g), d], x_ss.at[d, g], x_rs.at[d, g], moved(dx))

    def relay(g):
        for k, d, dx in ((0, 3, 1), (1, 1, 3)):
            taken(ra.at[four(g), d], x_rs.at[d, g])
            give(ra.at[two(g, k), d], ra.at[two(g, k), 2], x2_ss.at[k, g], x2_rs.at[k, g], moved(dx))

    def ffn(g):
        for k in range(2):
            taken(ra.at[two(g, k), 2], x2_rs.at[k, g])
        for i in range(g * NY, (g + 1) * NY):
            if i:
                taken(rb.at[i], db_rs.at[i])
            else:
                own[1].wait()

        @pl.loop(0, FFC // 256)
        def _(j):
            part = pl.ds(pl.multiple_of(j * 256, 256), 256)
            rows_a = ra[g * NY : (g + 1) * NY].reshape(ROWS, CA)
            rows_b = rb[g * NY : (g + 1) * NY].reshape(ROWS, CB)
            nt = ((1,), (1,))
            gate = dot(rows_a, wbuf[0, part, :CA], nt) + dot(rows_b, wbuf[0, part, CA:], nt)
            up = dot(rows_a, wbuf[1, part, :CA], nt) + dot(rows_b, wbuf[1, part, CA:], nt)
            hbuf[:, part] = (gate / (1.0 + jnp.exp(-gate)) * up).astype(bf16)

        for ref, first, width in ((tb, CA, CB), (ta, 0, CA)):
            @pl.loop(0, width // 768)
            def _(j):
                part = pl.ds(pl.multiple_of(j * 768, 256), 768)
                down = pl.ds(pl.multiple_of(first + j * 768, 256), 768)
                ref[g * NY : (g + 1) * NY, :, :, part] = (
                    dot(hbuf[...], wbuf[2, :, down]).astype(bf16).reshape(NY, NX, CAP, 768)
                )

    def sums(g):
        for k, dx in ((0, 1), (1, 3)):
            give(ta.at[two(g, k), 2], qa.at[k, pl.ds(2 * g, 2)], y_ss.at[0, k, g], y_rs.at[0, k, g], moved(dx))
        for k, d, v in ((1, 1, 0), (0, 3, 1)):
            give(ta.at[two(g, k), d], va.at[v, two(g, k)], y_ss.at[1, v, g], y_rs.at[1, v, g], moved(d))
        for i in range(g * NY, (g + 1) * NY):
            if i:
                give(tb.at[i], retb.at[me], bb_ss.at[i], bb_rs.at[me], moved(0, 0, i // NY, i % NY))
            else:
                retb[me] = tb[0]

    def pass_on(g):
        for k, d, v in ((0, 1, 0), (1, 3, 1)):
            taken(qa.at[k, pl.ds(2 * g, 2)], y_rs.at[0, k, g])
            for i in range(2):
                at = g * NY + 2 * k + i
                ta[at, d] = (ta[at, d].astype(f32) + qa[k, 2 * g + i].astype(f32)).astype(bf16)
            give(ta.at[two(g, k), d], va.at[v, two(g, k)], y_ss.at[2, v, g], y_rs.at[2, v, g], moved(d))

    def finish(g):
        for k, v in ((1, 0), (0, 1)):
            taken(va.at[v, two(g, k)], y_rs.at[1, v, g])
        for k, v in ((0, 0), (1, 1)):
            taken(va.at[v, two(g, k)], y_rs.at[2, v, g])
        for i in range(g * NY, (g + 1) * NY):
            total = (ta[i, 0].astype(f32) + va[0, i].astype(f32) + va[1, i].astype(f32)).astype(bf16)
            if i:
                ua[i] = total
                give(ua.at[i], reta.at[me], ba_ss.at[i], ba_rs.at[me], moved(0, 0, i // NY, i % NY))
            else:
                reta[me] = total

    forward(0)
    forward(1)
    relay(0)
    forward(2)
    relay(1)
    forward(3)
    relay(2)
    for copy in loads:
        copy.wait()
    for k in range(3):
        taken(wbuf.at[k, pl.ds(FFD, FFD)], w_rs.at[k])
    ffn(0)
    sums(0)
    relay(3)
    ffn(1)
    sums(1)
    pass_on(0)
    ffn(2)
    sums(2)
    pass_on(1)
    finish(0)
    ffn(3)
    sums(3)
    pass_on(2)
    finish(1)

    lanes = lax.broadcasted_iota(jnp.int32, (TOK, 2 * EXPERTS * CAP), 1).astype(f32)
    eights = lax.broadcasted_iota(jnp.int32, (TOK, EXPERTS), 1).astype(f32)
    later = lax.broadcasted_iota(jnp.int32, (TOK, TOK), 0) > lax.broadcasted_iota(jnp.int32, (TOK, TOK), 1)
    later = jnp.where(later, 1.0, 0.0).astype(bf16)

    def gate_rows(d):
        columns = jnp.concatenate([meta[d], jnp.zeros((120, 128), f32)], axis=0).T[:TOK]
        q0, q1 = columns[:, 0:1], columns[:, 1:2]
        names = jnp.where((eights == q0) | (eights == q1), 1.0, 0.0)
        ranks = dot(later, names.astype(bf16))
        mix = jnp.zeros((TOK, 2 * EXPERTS * CAP), f32)
        for q, gate in ((q0, columns[:, 2:3]), (q1, columns[:, 3:4])):
            at = q * (2 * CAP) + jnp.sum(jnp.where(eights == q, ranks, 0.0), axis=1, keepdims=True)
            mix = mix + jnp.where((lanes == at) | (lanes == at + CAP), gate, 0.0)
        high = mix.astype(bf16)
        return high, (mix - high.astype(f32)).astype(bf16)

    def mixture(gate, rows):
        return dot(gate[0], rows) + dot(gate[1], rows)

    gates = [gate_rows(d) for d in range(NX)]
    pass_on(3)
    finish(2)
    for dz, dy in plane:
        other = moved(0, 0, dz, dy)[2]
        taken(retb.at[other], bb_rs.at[other])
    for d in around:
        mixed[d, 0] = mixture(gates[d], retb[:, d].reshape(ROWS, CB)).astype(bf16)
        give(mixed.at[d, 0], mixed.at[(NX - d) % NX, 1], m_ss.at[d], m_rs.at[(NX - d) % NX], moved(d))
    finish(3)
    own_mix = mixture(gates[0], retb[:, 0].reshape(ROWS, CB))

    hot = (lax.broadcasted_iota(jnp.int32, (NSEQ, TOK), 0) == seg_ref[...]).astype(f32)
    count = jnp.broadcast_to(jnp.sum(hot, axis=1, keepdims=True), (NSEQ, 128))
    hot = hot.astype(bf16)

    def pool(embedded, part):
        emb_ref[:, part] = embedded
        sums = dot(hot, embedded)
        for i in range(PLANE):
            pb[i, :, part] = sums[2 * i : 2 * i + 2]

    for d in around:
        taken(mixed.at[d, 1], m_rs.at[d])
        own_mix = own_mix + mixed[d, 1].astype(f32)
    pool((tok_ref[:, CA:].astype(f32) + own_mix).astype(bf16), pl.ds(CA, CB))
    for dz, dy in plane:
        other = moved(0, 0, dz, dy)[2]
        taken(reta.at[other], ba_rs.at[other])

    @pl.loop(0, CA // 768)
    def _(j):
        part = pl.ds(pl.multiple_of(j * 768, 256), 768)
        rows = reta[:, :, part].reshape(ROWS, 768)
        pool((tok_ref[:, part].astype(f32) + mixture(gates[0], rows)).astype(bf16), part)

    for i in range(PLANE):
        pb[i, :, D:] = count[2 * i : 2 * i + 2]

    for dz, dy in plane:
        target = moved(0, 0, dz, dy)
        copy = remote(pb.at[target[2]], pr.at[me], p_ss.at[target[2]], p_rs.at[me], target)
        copy.start()
        sends.append(copy)
    pr[me] = pb[me]
    for dz, dy in plane:
        target = moved(0, 0, dz, dy)
        remote(pb.at[0], pr.at[target[2]], p_ss.at[0], p_rs.at[target[2]], target).wait_recv()
    p2[...] = jnp.sum(pr[...], axis=0)
    mine = x * 2 + c
    for k, (dx, dc) in enumerate(line):
        target = moved(dx, dc)
        copy = remote(p2, p2r.at[mine], p2_ss.at[k], p2_rs.at[mine], target)
        copy.start()
        sends.append(copy)
    p2r[mine] = p2[...]
    for k, (dx, dc) in enumerate(line):
        target = moved(dx, dc)
        other = target[0] * 2 + target[1]
        remote(p2, p2r.at[other], p2_ss.at[k], p2_rs.at[other], target).wait_recv()
    total = jnp.sum(p2r[...], axis=0)
    p3[me] = total[:, :D] / jnp.concatenate([total[:, D:]] * (D // 128), axis=1)
    for dz, dy in plane:
        target = moved(0, 0, dz, dy)
        copy = remote(p3.at[me], p3.at[me], p3_ss.at[target[2]], p3_rs.at[me], target)
        copy.start()
        sends.append(copy)
    for dz, dy in plane:
        target = moved(0, 0, dz, dy)
        remote(p3.at[target[2]], p3.at[target[2]], p3_ss.at[0], p3_rs.at[target[2]], target).wait_recv()
    for i in range(PLANE):
        pool_ref[2 * i : 2 * i + 2, :] = p3[i]
    for copy in sends:
        copy.wait_send()


def shards(tokens, routes, gates, segments, w_gate, w_up, w_down):
    vmem = pl.BlockSpec(memory_space=pltpu.VMEM)
    hbm = pl.BlockSpec(memory_space=pl.ANY)
    sem = pltpu.SemaphoreType.DMA
    return pl.pallas_call(
        kernel,
        name="moe",
        out_shape=(
            jax.ShapeDtypeStruct((TOK, D), bf16),
            jax.ShapeDtypeStruct((NSEQ, D), f32),
        ),
        in_specs=[vmem] * 4 + [hbm] * 3,
        out_specs=(vmem, vmem),
        scratch_shapes=[
            pltpu.VMEM((EXPERTS, CAP, CA), bf16),
            pltpu.VMEM((EXPERTS, NX, CAP, CB), bf16),
            pltpu.VMEM((3, FFC, D), bf16),
            pltpu.VMEM((PLANE, NX, CAP, CA), bf16),
            pltpu.VMEM((PLANE, NX, CAP, CB), bf16),
            pltpu.VMEM((ROWS, FFC), bf16),
            pltpu.VMEM((PLANE, NX, CAP, CA), bf16),
            pltpu.VMEM((PLANE, NX, CAP, CB), bf16),
            pltpu.VMEM((2, PLANE, CAP, CA), bf16),
            pltpu.VMEM((2, PLANE // 2, CAP, CA), bf16),
            pltpu.VMEM((PLANE, CAP, CA), bf16),
            pltpu.VMEM((PLANE, CAP, CA), bf16),
            pltpu.VMEM((PLANE, NX, CAP, CB), bf16),
            pltpu.VMEM((NX, TOK, CB), bf16),
            pltpu.VMEM((NX, 8, 128), f32),
            pltpu.VMEM((NX, 2, TOK, CB), bf16),
            pltpu.VMEM((PLANE, 2, PW), f32),
            pltpu.VMEM((PLANE, 2, PW), f32),
            pltpu.VMEM((2, PW), f32),
            pltpu.VMEM((8, 2, PW), f32),
            pltpu.VMEM((PLANE, 2, D), f32),
            sem((3,)), sem((3,)), sem((3,)), sem((2,)),
            sem((NX,)), sem((NX,)), sem((NX,)), sem((NX,)),
            sem((PLANE,)), sem((PLANE,)), sem((PLANE,)), sem((PLANE,)),
            sem((NX, NZ)), sem((NX, NZ)), sem((2, NZ)), sem((2, NZ)),
            sem((3, 2, NZ)), sem((3, 2, NZ)),
            sem((PLANE,)), sem((PLANE,)), sem((PLANE,)), sem((PLANE,)),
            sem((NX,)), sem((NX,)),
            sem((PLANE,)), sem((PLANE,)),
            sem((8,)), sem((8,)),
            sem((PLANE,)), sem((PLANE,)),
        ],
        compiler_params=pltpu.CompilerParams(
            collective_id=0, has_side_effects=True, vmem_limit_bytes=58 * 2**20
        ),
    )(
        tokens,
        routes.T,
        gates.T,
        segments[None, :],
        jnp.swapaxes(w_gate[0], 0, 1),
        jnp.swapaxes(w_up[0], 0, 1),
        w_down[0],
    )


def solution(mesh):
    placed = (
        P(("dp", "tensor", "expert"), None),
        P(("dp", "tensor", "expert"), None),
        P(("dp", "tensor", "expert"), None),
        P(("dp", "tensor", "expert")),
        P("expert", None, ("dp", "tensor")),
        P("expert", None, ("dp", "tensor")),
        P("expert", ("dp", "tensor"), None),
    )
    return jax.shard_map(
        shards,
        mesh=mesh,
        in_specs=placed,
        out_specs=(P(("dp", "tensor", "expert"), None), P()),
        check_vma=False,
    )
```

```python
import jax
import jax.numpy as jnp
from jax import lax
from jax.experimental import pallas as pl
from jax.experimental.pallas import tpu as pltpu
from jax.sharding import PartitionSpec as P

EXPERTS = 8
TOP = 2
CAP = 24
epsilon = 1e-06

NX = 4
NY = 4
NZ = 4
PLANE = NY * NZ
D = 2304
FFD = 480
FFC = 1024
TOK = 64
NSEQ = 32
ROWS = PLANE * CAP
CB = 768
CA = D - CB
PW = D + 128
MESH = pl.DeviceIdType.MESH
bf16 = jnp.bfloat16
f32 = jnp.float32


def place():
    expert = lax.axis_index("expert")
    return lax.axis_index("dp"), lax.axis_index("tensor"), expert // NY, expert % NY


def moved(dx=0, dc=0, dz=0, dy=0):
    x, c, z, y = place()
    return ((x + dx) % NX, (c + dc) % 2, ((z + dz) % NZ) * NY + (y + dy) % NY)


def dot(a, b, dims=((1,), (0,))):
    return lax.dot_general(a, b, (dims, ((), ())), preferred_element_type=f32)


def tiles(columns):
    return [(first, min(768, columns - first)) for first in range(0, columns, 768)]


def kernel(
    tok_ref, routes_ref, gates_ref, seg_ref, wg_ref, wu_ref, wd_ref, emb_ref, pool_ref,
    sa, sb, wbuf, ra, rb, hbuf, ta, tb, va, qa, ua, reta, retb, raw, meta, mixed, mbs, mbr, ps, pb, pr, p2, p2r, p3,
    w_ls, w_ss, w_rs, l_s, raw_ss, raw_rs, meta_ss, meta_rs, da_ss, da_rs, db_ss, db_rs, x_ss, x_rs, x2_ss, x2_rs,
    y_ss, y_rs, ba_ss, ba_rs, bb_ss, bb_rs, m_ss, m_rs, mb_ss, mb_rs, o_ss, o_rs, p_ss, p_rs, p2_ss, p2_rs, p3_ss, p3_rs,
):
    x, c, z, y = place()
    me = lax.axis_index("expert")
    plane = [(2, 2), (3, 2), (2, 3), (1, 2), (2, 1), (2, 0), (0, 2), (1, 1), (3, 3), (1, 3), (3, 1), (1, 0), (0, 3), (3, 0), (0, 1)]
    line = [(dx, dc) for dx in range(NX) for dc in range(2) if dx or dc]
    around = (1, 3, 2)
    sends = []

    def remote(src, dst, send, recv, target):
        return pltpu.make_async_remote_copy(
            src_ref=src, dst_ref=dst, send_sem=send, recv_sem=recv, device_id=target, device_id_type=MESH
        )

    def home(i):
        dz, dy = plane[i - 1]
        return moved(0, 0, NZ - dz, NY - dy)

    def give(src, dst, send, recv, target):
        copy = remote(src, dst, send, recv, target)
        copy.start()
        sends.append(copy)

    def taken(dst, recv):
        remote(dst, dst, recv, recv, moved(1)).wait_recv()

    barrier = pltpu.get_barrier_semaphore()
    for dz, dy in plane:
        pl.semaphore_signal(barrier, inc=1, device_id=moved(0, 0, dz, dy), device_id_type=MESH)
    for dx, dc in line:
        pl.semaphore_signal(barrier, inc=1, device_id=moved(dx, dc), device_id_type=MESH)

    weights = (wg_ref, wu_ref, wd_ref)
    loads = [pltpu.make_async_copy(w, wbuf.at[k, pl.ds(0, FFD)], w_ls.at[k]) for k, w in enumerate(weights)]
    for copy in loads:
        copy.start()

    meta[0] = jnp.concatenate(
        [
            jnp.concatenate(
                [routes_ref[...].astype(f32), gates_ref[...], seg_ref[...].astype(f32), jnp.zeros((3, TOK), f32)], axis=0
            ),
            jnp.full((8, 128 - TOK), -1.0, f32),
        ],
        axis=1,
    )
    experts = lax.broadcasted_iota(jnp.int32, (EXPERTS, 128), 0).astype(f32)
    earlier = lax.broadcasted_iota(jnp.int32, (128, 128), 0) < lax.broadcasted_iota(jnp.int32, (128, 128), 1)
    earlier = jnp.where(earlier, 1.0, 0.0).astype(bf16)
    slots = lax.broadcasted_iota(jnp.int32, (EXPERTS, CAP, TOK), 1).astype(f32)

    def spots_of(d):
        rows = meta[d]
        named = jnp.where((experts == rows[0:1]) | (experts == rows[1:2]), 1.0, 0.0)
        return jnp.where(named > 0.5, dot(named.astype(bf16), earlier), -1.0)

    def place_rows(spot):
        return jnp.where(slots == spot[:, None, :TOK], 1.0, 0.0).reshape(EXPERTS * CAP, TOK).astype(bf16)

    values = tok_ref[...].astype(f32)
    scale = lax.rsqrt(jnp.mean(values * values, axis=1, keepdims=True) + epsilon)
    normed = (values * scale).astype(bf16)
    raw[0] = normed[:, CA:]
    spots = [spots_of(0), None, None, None]
    placing = place_rows(spots[0])
    sa[...] = dot(placing, normed[:, :CA]).astype(bf16).reshape(EXPERTS, CAP, CA)

    pl.semaphore_wait(barrier, len(plane) + len(line))
    for dx in around:
        d = (NX - dx) % NX
        give(meta.at[0], meta.at[d], meta_ss.at[d], meta_rs.at[d], moved(dx))
        give(raw.at[0], raw.at[d], raw_ss.at[d], raw_rs.at[d], moved(dx))
    own = [pltpu.make_async_copy(sa.at[me // 2], ra.at[0, 0], l_s.at[0])]
    own[0].start()
    for back, (dz, dy) in enumerate(plane, 1):
        target = moved(0, 0, dz, dy)
        give(sa.at[target[2] // 2], ra.at[back, 0], da_ss.at[back], da_rs.at[back], target)
    own[0].wait()
    for k, (dx, d) in enumerate(((1, 3), (3, 1))):
        give(ra.at[0, 0], ra.at[0, d], o_ss.at[k], o_rs.at[k], moved(dx))
    for k, w in enumerate(weights):
        give(w, wbuf.at[k, pl.ds(FFD, FFD)], w_ss.at[k], w_rs.at[k], moved(0, 1))
    sb[:, 0] = dot(placing, raw[0]).astype(bf16).reshape(EXPERTS, CAP, CB)
    for d in around:
        taken(meta.at[d], meta_rs.at[d])
        taken(raw.at[d], raw_rs.at[d])
        spots[d] = spots_of(d)
        sb[:, d] = dot(place_rows(spots[d]), raw[d]).astype(bf16).reshape(EXPERTS, CAP, CB)
    own.append(pltpu.make_async_copy(sb.at[me // 2], rb.at[0], l_s.at[1]))
    own[1].start()
    for back, (dz, dy) in enumerate(plane, 1):
        target = moved(0, 0, dz, dy)
        give(sb.at[target[2] // 2], rb.at[back], db_ss.at[back], db_rs.at[back], target)
    info = jnp.concatenate([meta[d] for d in range(NX)], axis=1)
    lane = jnp.concatenate([jnp.where(s < 0.0, s, s + CAP * d) for d, s in enumerate(spots)], axis=1)
    names = jnp.concatenate([experts] * NX, axis=1)
    gate = jnp.where(names == info[0:1], info[2:3], 0.0) + jnp.where(names == info[1:2], info[3:4], 0.0)
    gate_high = gate.astype(bf16).astype(f32)
    to = lax.broadcasted_iota(jnp.int32, (128, NX * 128), 0).astype(f32)
    for e in range(EXPERTS):
        facts = jnp.concatenate(
            [
                gate_high[e : e + 1], gate[e : e + 1] - gate_high[e : e + 1], info[4:5],
                jnp.zeros((5, NX * 128), f32),
            ],
            axis=0,
        ).astype(bf16)
        hits = jnp.where(to == lane[e : e + 1], 1.0, 0.0).astype(bf16)
        mbs[e] = dot(facts, hits, ((1,), (1,)))
    mbr[0] = mbs[me // 2]
    for back, (dz, dy) in enumerate(plane, 1):
        target = moved(0, 0, dz, dy)
        give(mbs.at[target[2] // 2], mbr.at[back], mb_ss.at[back], mb_rs.at[back], target)
    wbuf[:, pl.ds(2 * FFD, FFC - 2 * FFD), :] = jnp.zeros((3, FFC - 2 * FFD, D), bf16)

    def four(g):
        return pl.ds(g * NY, NY)

    def two(g, k):
        return pl.ds(g * NY + 2 * k, 2)

    def fresh(g):
        return pl.ds(g * NY, NY) if g else pl.ds(1, NY - 1)

    def forward(g):
        for i in range(g * NY, (g + 1) * NY):
            if i:
                taken(ra.at[i, 0], da_rs.at[i])
        for dx, d in ((1, 3), (3, 1)):
            give(ra.at[fresh(g), 0], ra.at[fresh(g), d], x_ss.at[d, g], x_rs.at[d, g], moved(dx))

    def relay(g):
        for k, d, dx in ((0, 3, 1), (1, 1, 3)):
            taken(ra.at[fresh(g), d], x_rs.at[d, g])
            if g == 0:
                taken(ra.at[0, d], o_rs.at[k])
            give(ra.at[two(g, k), d], ra.at[two(g, k), 2], x2_ss.at[k, g], x2_rs.at[k, g], moved(dx))

    def ffn(g):
        for k in range(2):
            taken(ra.at[two(g, k), 2], x2_rs.at[k, g])
        for i in range(g * NY, (g + 1) * NY):
            if i:
                taken(rb.at[i], db_rs.at[i])
            else:
                own[1].wait()

        @pl.loop(0, FFC // 256)
        def _(j):
            part = pl.ds(pl.multiple_of(j * 256, 256), 256)
            rows_a = ra[g * NY : (g + 1) * NY].reshape(ROWS, CA)
            rows_b = rb[g * NY : (g + 1) * NY].reshape(ROWS, CB)
            nt = ((1,), (1,))
            gate = dot(rows_a, wbuf[0, part, :CA], nt) + dot(rows_b, wbuf[0, part, CA:], nt)
            up = dot(rows_a, wbuf[1, part, :CA], nt) + dot(rows_b, wbuf[1, part, CA:], nt)
            hbuf[:, part] = (gate / (1.0 + jnp.exp(-gate)) * up).astype(bf16)

        for ref, start, columns in ((tb, CA, CB), (ta, 0, CA)):
            for first, width in tiles(columns):
                down = slice(start + first, start + first + width)
                ref[g * NY : (g + 1) * NY, :, :, first : first + width] = (
                    dot(hbuf[...], wbuf[2, :, down]).astype(bf16).reshape(NY, NX, CAP, width)
                )

    sequence = lax.broadcasted_iota(jnp.int32, (NSEQ, 128), 0).astype(f32)

    def per_sequence(g):
        for i in range(g * NY, (g + 1) * NY):
            if i:
                taken(mbr.at[i], mb_rs.at[i])
            rows = mbr[i]
            hit = sequence == rows[2:3]
            weigh = jnp.concatenate([jnp.where(hit, rows[0:1], 0.0), jnp.where(hit, rows[1:2], 0.0)], axis=0)
            weigh = weigh[:, : NX * CAP].astype(bf16)
            for ref, part in ((ta, slice(0, CA)), (tb, slice(CA, D))):
                both = dot(weigh, ref[i].reshape(NX * CAP, ref.shape[3]))
                ps[:, part] += both[:NSEQ] + both[NSEQ:]

    def sums(g):
        for k, dx in ((0, 1), (1, 3)):
            give(ta.at[two(g, k), 2], qa.at[k, pl.ds(2 * g, 2)], y_ss.at[0, k, g], y_rs.at[0, k, g], moved(dx))
        for k, d, v in ((1, 1, 0), (0, 3, 1)):
            give(ta.at[two(g, k), d], va.at[v, two(g, k)], y_ss.at[1, v, g], y_rs.at[1, v, g], moved(d))
        for i in range(g * NY, (g + 1) * NY):
            if i:
                give(tb.at[i], retb.at[me], bb_ss.at[i], bb_rs.at[me], home(i))
            else:
                retb[me] = tb[0]

    def pass_on(g):
        for k, d, v in ((0, 1, 0), (1, 3, 1)):
            taken(qa.at[k, pl.ds(2 * g, 2)], y_rs.at[0, k, g])
            for i in range(2):
                at = g * NY + 2 * k + i
                ta[at, d] = (ta[at, d].astype(f32) + qa[k, 2 * g + i].astype(f32)).astype(bf16)
            give(ta.at[two(g, k), d], va.at[v, two(g, k)], y_ss.at[2, v, g], y_rs.at[2, v, g], moved(d))

    def finish(g):
        for k, v in ((1, 0), (0, 1)):
            taken(va.at[v, two(g, k)], y_rs.at[1, v, g])
        for k, v in ((0, 0), (1, 1)):
            taken(va.at[v, two(g, k)], y_rs.at[2, v, g])
        for i in range(g * NY, (g + 1) * NY):
            total = (ta[i, 0].astype(f32) + va[0, i].astype(f32) + va[1, i].astype(f32)).astype(bf16)
            if i:
                ua[i] = total
                give(ua.at[i], reta.at[me], ba_ss.at[i], ba_rs.at[me], home(i))
            else:
                reta[me] = total

    forward(0)
    forward(1)
    relay(0)
    forward(2)
    relay(1)
    forward(3)
    relay(2)
    for copy in loads:
        copy.wait()
    for k in range(3):
        taken(wbuf.at[k, pl.ds(FFD, FFD)], w_rs.at[k])
    hot = (lax.broadcasted_iota(jnp.int32, (NSEQ, TOK), 0) == seg_ref[...]).astype(f32)
    count = jnp.broadcast_to(jnp.sum(hot, axis=1, keepdims=True), (NSEQ, 128))
    ps[...] = dot(hot.astype(bf16), tok_ref[...])
    ffn(0)
    sums(0)
    relay(3)
    per_sequence(0)
    ffn(1)
    sums(1)
    pass_on(0)
    per_sequence(1)
    ffn(2)
    sums(2)
    pass_on(1)
    finish(0)
    per_sequence(2)
    ffn(3)
    sums(3)
    per_sequence(3)
    for i in range(PLANE):
        pb[i, :, :D] = ps[2 * i : 2 * i + 2, :]
        pb[i, :, D:] = count[2 * i : 2 * i + 2]
    for dz, dy in plane:
        target = moved(0, 0, dz, dy)
        give(pb.at[target[2]], pr.at[me], p_ss.at[target[2]], p_rs.at[me], target)
    pr[me] = pb[me]
    pass_on(2)
    finish(1)

    lanes = lax.broadcasted_iota(jnp.int32, (TOK, 2 * EXPERTS * CAP), 1).astype(f32)
    eights = lax.broadcasted_iota(jnp.int32, (TOK, EXPERTS), 1).astype(f32)
    later = lax.broadcasted_iota(jnp.int32, (TOK, TOK), 0) > lax.broadcasted_iota(jnp.int32, (TOK, TOK), 1)
    later = jnp.where(later, 1.0, 0.0).astype(bf16)

    def gate_rows(d):
        columns = jnp.concatenate([meta[d], jnp.zeros((120, 128), f32)], axis=0).T[:TOK]
        q0, q1 = columns[:, 0:1], columns[:, 1:2]
        names = jnp.where((eights == q0) | (eights == q1), 1.0, 0.0)
        ranks = dot(later, names.astype(bf16))
        mix = jnp.zeros((TOK, 2 * EXPERTS * CAP), f32)
        for q, gate in ((q0, columns[:, 2:3]), (q1, columns[:, 3:4])):
            at = q * (2 * CAP) + jnp.sum(jnp.where(eights == q, ranks, 0.0), axis=1, keepdims=True)
            mix = mix + jnp.where((lanes == at) | (lanes == at + CAP), gate, 0.0)
        high = mix.astype(bf16)
        return high, (mix - high.astype(f32)).astype(bf16)

    def mixture(gate, rows):
        return dot(gate[0], rows) + dot(gate[1], rows)

    gates = [gate_rows(d) for d in range(NX)]
    for dz, dy in plane:
        other = moved(0, 0, dz, dy)[2]
        taken(pr.at[other], p_rs.at[other])
    p2[...] = jnp.sum(pr[...], axis=0)
    mine = x * 2 + c
    for k, (dx, dc) in enumerate(line):
        give(p2, p2r.at[mine], p2_ss.at[k], p2_rs.at[mine], moved(dx, dc))
    p2r[mine] = p2[...]
    pass_on(3)
    finish(2)
    for dz, dy in plane:
        other = moved(0, 0, dz, dy)[2]
        taken(retb.at[other], bb_rs.at[other])
    for d in around:
        mixed[d, 0] = mixture(gates[d], retb[:, d].reshape(ROWS, CB)).astype(bf16)
        give(mixed.at[d, 0], mixed.at[(NX - d) % NX, 1], m_ss.at[d], m_rs.at[(NX - d) % NX], moved(d))
    for dx, dc in line:
        target = moved(dx, dc)
        other = target[0] * 2 + target[1]
        taken(p2r.at[other], p2_rs.at[other])
    total = jnp.sum(p2r[...], axis=0)
    p3[me] = total[:, :D] / jnp.concatenate([total[:, D:]] * (D // 128), axis=1)
    for dz, dy in plane:
        target = moved(0, 0, dz, dy)
        give(p3.at[me], p3.at[me], p3_ss.at[target[2]], p3_rs.at[me], target)
    finish(3)
    own_mix = mixture(gates[0], retb[:, 0].reshape(ROWS, CB))
    for d in around:
        taken(mixed.at[d, 1], m_rs.at[d])
        own_mix = own_mix + mixed[d, 1].astype(f32)
    emb_ref[:, CA:] = (tok_ref[:, CA:].astype(f32) + own_mix).astype(bf16)
    for dz, dy in plane:
        other = moved(0, 0, dz, dy)[2]
        taken(p3.at[other], p3_rs.at[other])
    for i in range(PLANE):
        pool_ref[2 * i : 2 * i + 2, :] = p3[i]
    for dz, dy in plane:
        other = moved(0, 0, dz, dy)[2]
        taken(reta.at[other], ba_rs.at[other])
    for first, width in tiles(CA):
        part = slice(first, first + width)
        rows = reta[:, :, part].reshape(ROWS, width)
        emb_ref[:, part] = (tok_ref[:, part].astype(f32) + mixture(gates[0], rows)).astype(bf16)
    for copy in sends:
        copy.wait_send()


def shards(tokens, routes, gates, segments, w_gate, w_up, w_down):
    vmem = pl.BlockSpec(memory_space=pltpu.VMEM)
    hbm = pl.BlockSpec(memory_space=pl.ANY)
    sem = pltpu.SemaphoreType.DMA
    return pl.pallas_call(
        kernel,
        name="moe",
        out_shape=(
            jax.ShapeDtypeStruct((TOK, D), bf16),
            jax.ShapeDtypeStruct((NSEQ, D), f32),
        ),
        in_specs=[vmem] * 4 + [hbm] * 3,
        out_specs=(vmem, vmem),
        scratch_shapes=[
            pltpu.VMEM((EXPERTS, CAP, CA), bf16),
            pltpu.VMEM((EXPERTS, NX, CAP, CB), bf16),
            pltpu.VMEM((3, FFC, D), bf16),
            pltpu.VMEM((PLANE, NX, CAP, CA), bf16),
            pltpu.VMEM((PLANE, NX, CAP, CB), bf16),
            pltpu.VMEM((ROWS, FFC), bf16),
            pltpu.VMEM((PLANE, NX, CAP, CA), bf16),
            pltpu.VMEM((PLANE, NX, CAP, CB), bf16),
            pltpu.VMEM((2, PLANE, CAP, CA), bf16),
            pltpu.VMEM((2, PLANE // 2, CAP, CA), bf16),
            pltpu.VMEM((PLANE, CAP, CA), bf16),
            pltpu.VMEM((PLANE, CAP, CA), bf16),
            pltpu.VMEM((PLANE, NX, CAP, CB), bf16),
            pltpu.VMEM((NX, TOK, CB), bf16),
            pltpu.VMEM((NX, 8, 128), f32),
            pltpu.VMEM((NX, 2, TOK, CB), bf16),
            pltpu.VMEM((EXPERTS, 8, 128), f32),
            pltpu.VMEM((PLANE, 8, 128), f32),
            pltpu.VMEM((NSEQ, D), f32),
            pltpu.VMEM((PLANE, 2, PW), f32),
            pltpu.VMEM((PLANE, 2, PW), f32),
            pltpu.VMEM((2, PW), f32),
            pltpu.VMEM((8, 2, PW), f32),
            pltpu.VMEM((PLANE, 2, D), f32),
            sem((3,)), sem((3,)), sem((3,)), sem((2,)),
            sem((NX,)), sem((NX,)), sem((NX,)), sem((NX,)),
            sem((PLANE,)), sem((PLANE,)), sem((PLANE,)), sem((PLANE,)),
            sem((NX, NZ)), sem((NX, NZ)), sem((2, NZ)), sem((2, NZ)),
            sem((3, 2, NZ)), sem((3, 2, NZ)),
            sem((PLANE,)), sem((PLANE,)), sem((PLANE,)), sem((PLANE,)),
            sem((NX,)), sem((NX,)),
            sem((PLANE,)), sem((PLANE,)), sem((2,)), sem((2,)),
            sem((PLANE,)), sem((PLANE,)),
            sem((8,)), sem((8,)),
            sem((PLANE,)), sem((PLANE,)),
        ],
        compiler_params=pltpu.CompilerParams(
            collective_id=0, has_side_effects=True, vmem_limit_bytes=58 * 2**20
        ),
    )(
        tokens,
        routes.T,
        gates.T,
        segments[None, :],
        jnp.swapaxes(w_gate[0], 0, 1),
        jnp.swapaxes(w_up[0], 0, 1),
        w_down[0],
    )


def solution(mesh):
    placed = (
        P(("dp", "tensor", "expert"), None),
        P(("dp", "tensor", "expert"), None),
        P(("dp", "tensor", "expert"), None),
        P(("dp", "tensor", "expert")),
        P("expert", None, ("dp", "tensor")),
        P("expert", None, ("dp", "tensor")),
        P("expert", ("dp", "tensor"), None),
    )
    return jax.shard_map(
        shards,
        mesh=mesh,
        in_specs=placed,
        out_specs=(P(("dp", "tensor", "expert"), None), P()),
        check_vma=False,
    )
```

```python
import jax
import jax.numpy as jnp
from jax import lax
from jax.experimental import pallas as pl
from jax.experimental.pallas import tpu as pltpu
from jax.sharding import PartitionSpec as P

EXPERTS = 8
TOP = 2
CAP = 24
epsilon = 1e-06

NX = 4
NY = 4
NZ = 4
PLANE = NY * NZ
D = 2304
FFD = 480
FFC = 1024
TOK = 64
NSEQ = 32
ROWS = PLANE * CAP
CB = 768
CA = D - CB
PW = D + 128
MESH = pl.DeviceIdType.MESH
bf16 = jnp.bfloat16
f32 = jnp.float32


def place():
    expert = lax.axis_index("expert")
    return lax.axis_index("dp"), lax.axis_index("tensor"), expert // NY, expert % NY


def moved(dx=0, dc=0, dz=0, dy=0):
    x, c, z, y = place()
    return ((x + dx) % NX, (c + dc) % 2, ((z + dz) % NZ) * NY + (y + dy) % NY)


def dot(a, b, dims=((1,), (0,))):
    return lax.dot_general(a, b, (dims, ((), ())), preferred_element_type=f32)


def tiles(columns):
    return [(first, min(768, columns - first)) for first in range(0, columns, 768)]


def kernel(
    tok_ref, routes_ref, gates_ref, seg_ref, wg_ref, wu_ref, wd_ref, emb_ref, pool_ref,
    sa, sb, wbuf, ra, rb, hbuf, ta, tb, va, qa, ua, reta, retb, raw, meta, mixed, mbs, mbr, ps, pb, pr, p2, p2r, p3,
    w_ls, w_ss, w_rs, l_s, raw_ss, raw_rs, meta_ss, meta_rs, da_ss, da_rs, db_ss, db_rs, x_ss, x_rs, x2_ss, x2_rs,
    y_ss, y_rs, ba_ss, ba_rs, bb_ss, bb_rs, m_ss, m_rs, mb_ss, mb_rs, o_ss, o_rs, p_ss, p_rs, p2_ss, p2_rs, p3_ss, p3_rs,
):
    x, c, z, y = place()
    me = lax.axis_index("expert")
    plane = [(1, 1), (3, 3), (2, 2), (1, 3), (3, 1), (2, 0), (0, 2), (3, 2), (2, 3), (1, 2), (2, 1), (1, 0), (0, 3), (3, 0), (0, 1)]
    line = [(dx, dc) for dx in range(NX) for dc in range(2) if dx or dc]
    around = (1, 3, 2)
    sends = []

    def remote(src, dst, send, recv, target):
        return pltpu.make_async_remote_copy(
            src_ref=src, dst_ref=dst, send_sem=send, recv_sem=recv, device_id=target, device_id_type=MESH
        )

    def home(i):
        dz, dy = plane[i - 1]
        return moved(0, 0, NZ - dz, NY - dy)

    def give(src, dst, send, recv, target):
        copy = remote(src, dst, send, recv, target)
        copy.start()
        sends.append(copy)

    def taken(dst, recv):
        remote(dst, dst, recv, recv, moved(1)).wait_recv()

    barrier = pltpu.get_barrier_semaphore()
    for dz, dy in plane:
        pl.semaphore_signal(barrier, inc=1, device_id=moved(0, 0, dz, dy), device_id_type=MESH)
    for dx, dc in line:
        pl.semaphore_signal(barrier, inc=1, device_id=moved(dx, dc), device_id_type=MESH)

    weights = (wg_ref, wu_ref, wd_ref)
    loads = [pltpu.make_async_copy(w, wbuf.at[k, pl.ds(0, FFD)], w_ls.at[k]) for k, w in enumerate(weights)]
    for copy in loads:
        copy.start()

    meta[0] = jnp.concatenate(
        [
            jnp.concatenate(
                [routes_ref[...].astype(f32), gates_ref[...], seg_ref[...].astype(f32), jnp.zeros((3, TOK), f32)], axis=0
            ),
            jnp.full((8, 128 - TOK), -1.0, f32),
        ],
        axis=1,
    )
    experts = lax.broadcasted_iota(jnp.int32, (EXPERTS, 128), 0).astype(f32)
    earlier = lax.broadcasted_iota(jnp.int32, (128, 128), 0) < lax.broadcasted_iota(jnp.int32, (128, 128), 1)
    earlier = jnp.where(earlier, 1.0, 0.0).astype(bf16)
    slots = lax.broadcasted_iota(jnp.int32, (EXPERTS, CAP, TOK), 1).astype(f32)

    def spots_of(d):
        rows = meta[d]
        named = jnp.where((experts == rows[0:1]) | (experts == rows[1:2]), 1.0, 0.0)
        return jnp.where(named > 0.5, dot(named.astype(bf16), earlier), -1.0)

    def place_rows(spot):
        return jnp.where(slots == spot[:, None, :TOK], 1.0, 0.0).reshape(EXPERTS * CAP, TOK).astype(bf16)

    values = tok_ref[...].astype(f32)
    scale = lax.rsqrt(jnp.mean(values * values, axis=1, keepdims=True) + epsilon)
    normed = (values * scale).astype(bf16)
    raw[0] = normed[:, CA:]
    spots = [spots_of(0), None, None, None]
    placing = place_rows(spots[0])
    sa[...] = dot(placing, normed[:, :CA]).astype(bf16).reshape(EXPERTS, CAP, CA)

    pl.semaphore_wait(barrier, len(plane) + len(line))
    for dx in around:
        d = (NX - dx) % NX
        give(meta.at[0], meta.at[d], meta_ss.at[d], meta_rs.at[d], moved(dx))
        give(raw.at[0], raw.at[d], raw_ss.at[d], raw_rs.at[d], moved(dx))
    own = [pltpu.make_async_copy(sa.at[me // 2], ra.at[0, 0], l_s.at[0])]
    own[0].start()
    for back, (dz, dy) in enumerate(plane, 1):
        target = moved(0, 0, dz, dy)
        give(sa.at[target[2] // 2], ra.at[back, 0], da_ss.at[back], da_rs.at[back], target)
    own[0].wait()
    for k, (dx, d) in enumerate(((1, 3), (3, 1))):
        give(ra.at[0, 0], ra.at[0, d], o_ss.at[k], o_rs.at[k], moved(dx))
    for k, w in enumerate(weights):
        give(w, wbuf.at[k, pl.ds(FFD, FFD)], w_ss.at[k], w_rs.at[k], moved(0, 1))
    sb[:, 0] = dot(placing, raw[0]).astype(bf16).reshape(EXPERTS, CAP, CB)
    for d in around:
        taken(meta.at[d], meta_rs.at[d])
        taken(raw.at[d], raw_rs.at[d])
        spots[d] = spots_of(d)
        sb[:, d] = dot(place_rows(spots[d]), raw[d]).astype(bf16).reshape(EXPERTS, CAP, CB)
    own.append(pltpu.make_async_copy(sb.at[me // 2], rb.at[0], l_s.at[1]))
    own[1].start()
    def offer(g):
        for back in range(max(1, g * NY), (g + 1) * NY):
            target = moved(0, 0, *plane[back - 1])
            give(sb.at[target[2] // 2], rb.at[back], db_ss.at[back], db_rs.at[back], target)

    offer(0)
    offer(1)
    info = jnp.concatenate([meta[d] for d in range(NX)], axis=1)
    lane = jnp.concatenate([jnp.where(s < 0.0, s, s + CAP * d) for d, s in enumerate(spots)], axis=1)
    names = jnp.concatenate([experts] * NX, axis=1)
    gate = jnp.where(names == info[0:1], info[2:3], 0.0) + jnp.where(names == info[1:2], info[3:4], 0.0)
    gate_high = gate.astype(bf16).astype(f32)
    to = lax.broadcasted_iota(jnp.int32, (128, NX * 128), 0).astype(f32)
    for e in range(EXPERTS):
        facts = jnp.concatenate(
            [
                gate_high[e : e + 1], gate[e : e + 1] - gate_high[e : e + 1], info[4:5],
                jnp.zeros((5, NX * 128), f32),
            ],
            axis=0,
        ).astype(bf16)
        hits = jnp.where(to == lane[e : e + 1], 1.0, 0.0).astype(bf16)
        mbs[e] = dot(facts, hits, ((1,), (1,)))
    mbr[0] = mbs[me // 2]
    for back, (dz, dy) in enumerate(plane, 1):
        target = moved(0, 0, dz, dy)
        give(mbs.at[target[2] // 2], mbr.at[back], mb_ss.at[back], mb_rs.at[back], target)
    wbuf[:, pl.ds(2 * FFD, FFC - 2 * FFD), :] = jnp.zeros((3, FFC - 2 * FFD, D), bf16)

    def four(g):
        return pl.ds(g * NY, NY)

    def two(g, k):
        return pl.ds(g * NY + 2 * k, 2)

    def fresh(g):
        return pl.ds(g * NY, NY) if g else pl.ds(1, NY - 1)

    def forward(g):
        for i in range(g * NY, (g + 1) * NY):
            if i:
                taken(ra.at[i, 0], da_rs.at[i])
        for dx, d in ((1, 3), (3, 1)):
            give(ra.at[fresh(g), 0], ra.at[fresh(g), d], x_ss.at[d, g], x_rs.at[d, g], moved(dx))

    def relay(g):
        for k, d, dx in ((0, 3, 1), (1, 1, 3)):
            taken(ra.at[fresh(g), d], x_rs.at[d, g])
            if g == 0:
                taken(ra.at[0, d], o_rs.at[k])
            give(ra.at[two(g, k), d], ra.at[two(g, k), 2], x2_ss.at[k, g], x2_rs.at[k, g], moved(dx))

    def ffn(g):
        for k in range(2):
            taken(ra.at[two(g, k), 2], x2_rs.at[k, g])
        for i in range(g * NY, (g + 1) * NY):
            if i:
                taken(rb.at[i], db_rs.at[i])
            else:
                own[1].wait()

        @pl.loop(0, FFC // 256)
        def _(j):
            part = pl.ds(pl.multiple_of(j * 256, 256), 256)
            rows_a = ra[g * NY : (g + 1) * NY].reshape(ROWS, CA)
            rows_b = rb[g * NY : (g + 1) * NY].reshape(ROWS, CB)
            nt = ((1,), (1,))
            gate = dot(rows_a, wbuf[0, part, :CA], nt) + dot(rows_b, wbuf[0, part, CA:], nt)
            up = dot(rows_a, wbuf[1, part, :CA], nt) + dot(rows_b, wbuf[1, part, CA:], nt)
            hbuf[:, part] = (gate / (1.0 + jnp.exp(-gate)) * up).astype(bf16)

        for ref, start, columns in ((tb, CA, CB), (ta, 0, CA)):
            for first, width in tiles(columns):
                down = slice(start + first, start + first + width)
                ref[g * NY : (g + 1) * NY, :, :, first : first + width] = (
                    dot(hbuf[...], wbuf[2, :, down]).astype(bf16).reshape(NY, NX, CAP, width)
                )

    sequence = lax.broadcasted_iota(jnp.int32, (NSEQ, 128), 0).astype(f32)

    def per_sequence(g):
        for i in range(g * NY, (g + 1) * NY):
            if i:
                taken(mbr.at[i], mb_rs.at[i])
            rows = mbr[i]
            hit = sequence == rows[2:3]
            weigh = jnp.concatenate([jnp.where(hit, rows[0:1], 0.0), jnp.where(hit, rows[1:2], 0.0)], axis=0)
            weigh = weigh[:, : NX * CAP].astype(bf16)
            for ref, part in ((ta, slice(0, CA)), (tb, slice(CA, D))):
                both = dot(weigh, ref[i].reshape(NX * CAP, ref.shape[3]))
                ps[:, part] += both[:NSEQ] + both[NSEQ:]

    def sums(g):
        for k, dx in ((0, 1), (1, 3)):
            give(ta.at[two(g, k), 2], qa.at[k, pl.ds(2 * g, 2)], y_ss.at[0, k, g], y_rs.at[0, k, g], moved(dx))
        for k, d, v in ((1, 1, 0), (0, 3, 1)):
            give(ta.at[two(g, k), d], va.at[v, two(g, k)], y_ss.at[1, v, g], y_rs.at[1, v, g], moved(d))
        for i in range(g * NY, (g + 1) * NY):
            if i:
                give(tb.at[i], retb.at[me], bb_ss.at[i], bb_rs.at[me], home(i))
            else:
                retb[me] = tb[0]

    def pass_on(g):
        for k, d, v in ((0, 1, 0), (1, 3, 1)):
            taken(qa.at[k, pl.ds(2 * g, 2)], y_rs.at[0, k, g])
            for i in range(2):
                at = g * NY + 2 * k + i
                ta[at, d] = (ta[at, d].astype(f32) + qa[k, 2 * g + i].astype(f32)).astype(bf16)
            give(ta.at[two(g, k), d], va.at[v, two(g, k)], y_ss.at[2, v, g], y_rs.at[2, v, g], moved(d))

    def finish(g):
        for k, v in ((1, 0), (0, 1)):
            taken(va.at[v, two(g, k)], y_rs.at[1, v, g])
        for k, v in ((0, 0), (1, 1)):
            taken(va.at[v, two(g, k)], y_rs.at[2, v, g])
        for i in range(g * NY, (g + 1) * NY):
            total = (ta[i, 0].astype(f32) + va[0, i].astype(f32) + va[1, i].astype(f32)).astype(bf16)
            if i:
                ua[i] = total
                give(ua.at[i], reta.at[me], ba_ss.at[i], ba_rs.at[me], home(i))
            else:
                reta[me] = total

    forward(0)
    forward(1)
    offer(2)
    relay(0)
    forward(2)
    offer(3)
    relay(1)
    forward(3)
    relay(2)
    for copy in loads:
        copy.wait()
    for k in range(3):
        taken(wbuf.at[k, pl.ds(FFD, FFD)], w_rs.at[k])
    hot = (lax.broadcasted_iota(jnp.int32, (NSEQ, TOK), 0) == seg_ref[...]).astype(f32)
    count = jnp.broadcast_to(jnp.sum(hot, axis=1, keepdims=True), (NSEQ, 128))
    ps[...] = dot(hot.astype(bf16), tok_ref[...])
    ffn(0)
    sums(0)
    relay(3)
    per_sequence(0)
    ffn(1)
    sums(1)
    pass_on(0)
    per_sequence(1)
    ffn(2)
    sums(2)
    pass_on(1)
    finish(0)
    per_sequence(2)
    ffn(3)
    sums(3)
    per_sequence(3)
    for i in range(PLANE):
        pb[i, :, :D] = ps[2 * i : 2 * i + 2, :]
        pb[i, :, D:] = count[2 * i : 2 * i + 2]
    for dz, dy in plane:
        target = moved(0, 0, dz, dy)
        give(pb.at[target[2]], pr.at[me], p_ss.at[target[2]], p_rs.at[me], target)
    pr[me] = pb[me]
    pass_on(2)
    finish(1)

    lanes = lax.broadcasted_iota(jnp.int32, (TOK, 2 * EXPERTS * CAP), 1).astype(f32)
    eights = lax.broadcasted_iota(jnp.int32, (TOK, EXPERTS), 1).astype(f32)
    later = lax.broadcasted_iota(jnp.int32, (TOK, TOK), 0) > lax.broadcasted_iota(jnp.int32, (TOK, TOK), 1)
    later = jnp.where(later, 1.0, 0.0).astype(bf16)

    def gate_rows(d):
        columns = jnp.concatenate([meta[d], jnp.zeros((120, 128), f32)], axis=0).T[:TOK]
        q0, q1 = columns[:, 0:1], columns[:, 1:2]
        names = jnp.where((eights == q0) | (eights == q1), 1.0, 0.0)
        ranks = dot(later, names.astype(bf16))
        mix = jnp.zeros((TOK, 2 * EXPERTS * CAP), f32)
        for q, gate in ((q0, columns[:, 2:3]), (q1, columns[:, 3:4])):
            at = q * (2 * CAP) + jnp.sum(jnp.where(eights == q, ranks, 0.0), axis=1, keepdims=True)
            mix = mix + jnp.where((lanes == at) | (lanes == at + CAP), gate, 0.0)
        high = mix.astype(bf16)
        return high, (mix - high.astype(f32)).astype(bf16)

    def mixture(gate, rows):
        return dot(gate[0], rows) + dot(gate[1], rows)

    gates = [gate_rows(d) for d in range(NX)]
    for dz, dy in plane:
        other = moved(0, 0, dz, dy)[2]
        taken(pr.at[other], p_rs.at[other])
    p2[...] = jnp.sum(pr[...], axis=0)
    mine = x * 2 + c
    for k, (dx, dc) in enumerate(line):
        give(p2, p2r.at[mine], p2_ss.at[k], p2_rs.at[mine], moved(dx, dc))
    p2r[mine] = p2[...]
    pass_on(3)
    finish(2)
    for dz, dy in plane:
        other = moved(0, 0, dz, dy)[2]
        taken(retb.at[other], bb_rs.at[other])
    for d in around:
        mixed[d, 0] = mixture(gates[d], retb[:, d].reshape(ROWS, CB)).astype(bf16)
        give(mixed.at[d, 0], mixed.at[(NX - d) % NX, 1], m_ss.at[d], m_rs.at[(NX - d) % NX], moved(d))
    for dx, dc in line:
        target = moved(dx, dc)
        other = target[0] * 2 + target[1]
        taken(p2r.at[other], p2_rs.at[other])
    total = jnp.sum(p2r[...], axis=0)
    p3[me] = total[:, :D] / jnp.concatenate([total[:, D:]] * (D // 128), axis=1)
    for dz, dy in plane:
        target = moved(0, 0, dz, dy)
        give(p3.at[me], p3.at[me], p3_ss.at[target[2]], p3_rs.at[me], target)
    finish(3)
    own_mix = mixture(gates[0], retb[:, 0].reshape(ROWS, CB))
    for d in around:
        taken(mixed.at[d, 1], m_rs.at[d])
        own_mix = own_mix + mixed[d, 1].astype(f32)
    emb_ref[:, CA:] = (tok_ref[:, CA:].astype(f32) + own_mix).astype(bf16)
    for dz, dy in plane:
        other = moved(0, 0, dz, dy)[2]
        taken(p3.at[other], p3_rs.at[other])
    for i in range(PLANE):
        pool_ref[2 * i : 2 * i + 2, :] = p3[i]
    for dz, dy in plane:
        other = moved(0, 0, dz, dy)[2]
        taken(reta.at[other], ba_rs.at[other])
    for first, width in tiles(CA):
        part = slice(first, first + width)
        rows = reta[:, :, part].reshape(ROWS, width)
        emb_ref[:, part] = (tok_ref[:, part].astype(f32) + mixture(gates[0], rows)).astype(bf16)
    for copy in sends:
        copy.wait_send()


def shards(tokens, routes, gates, segments, w_gate, w_up, w_down):
    vmem = pl.BlockSpec(memory_space=pltpu.VMEM)
    hbm = pl.BlockSpec(memory_space=pl.ANY)
    sem = pltpu.SemaphoreType.DMA
    return pl.pallas_call(
        kernel,
        name="moe",
        out_shape=(
            jax.ShapeDtypeStruct((TOK, D), bf16),
            jax.ShapeDtypeStruct((NSEQ, D), f32),
        ),
        in_specs=[vmem] * 4 + [hbm] * 3,
        out_specs=(vmem, vmem),
        scratch_shapes=[
            pltpu.VMEM((EXPERTS, CAP, CA), bf16),
            pltpu.VMEM((EXPERTS, NX, CAP, CB), bf16),
            pltpu.VMEM((3, FFC, D), bf16),
            pltpu.VMEM((PLANE, NX, CAP, CA), bf16),
            pltpu.VMEM((PLANE, NX, CAP, CB), bf16),
            pltpu.VMEM((ROWS, FFC), bf16),
            pltpu.VMEM((PLANE, NX, CAP, CA), bf16),
            pltpu.VMEM((PLANE, NX, CAP, CB), bf16),
            pltpu.VMEM((2, PLANE, CAP, CA), bf16),
            pltpu.VMEM((2, PLANE // 2, CAP, CA), bf16),
            pltpu.VMEM((PLANE, CAP, CA), bf16),
            pltpu.VMEM((PLANE, CAP, CA), bf16),
            pltpu.VMEM((PLANE, NX, CAP, CB), bf16),
            pltpu.VMEM((NX, TOK, CB), bf16),
            pltpu.VMEM((NX, 8, 128), f32),
            pltpu.VMEM((NX, 2, TOK, CB), bf16),
            pltpu.VMEM((EXPERTS, 8, 128), f32),
            pltpu.VMEM((PLANE, 8, 128), f32),
            pltpu.VMEM((NSEQ, D), f32),
            pltpu.VMEM((PLANE, 2, PW), f32),
            pltpu.VMEM((PLANE, 2, PW), f32),
            pltpu.VMEM((2, PW), f32),
            pltpu.VMEM((8, 2, PW), f32),
            pltpu.VMEM((PLANE, 2, D), f32),
            sem((3,)), sem((3,)), sem((3,)), sem((2,)),
            sem((NX,)), sem((NX,)), sem((NX,)), sem((NX,)),
            sem((PLANE,)), sem((PLANE,)), sem((PLANE,)), sem((PLANE,)),
            sem((NX, NZ)), sem((NX, NZ)), sem((2, NZ)), sem((2, NZ)),
            sem((3, 2, NZ)), sem((3, 2, NZ)),
            sem((PLANE,)), sem((PLANE,)), sem((PLANE,)), sem((PLANE,)),
            sem((NX,)), sem((NX,)),
            sem((PLANE,)), sem((PLANE,)), sem((2,)), sem((2,)),
            sem((PLANE,)), sem((PLANE,)),
            sem((8,)), sem((8,)),
            sem((PLANE,)), sem((PLANE,)),
        ],
        compiler_params=pltpu.CompilerParams(
            collective_id=0, has_side_effects=True, vmem_limit_bytes=58 * 2**20
        ),
    )(
        tokens,
        routes.T,
        gates.T,
        segments[None, :],
        jnp.swapaxes(w_gate[0], 0, 1),
        jnp.swapaxes(w_up[0], 0, 1),
        w_down[0],
    )


def solution(mesh):
    placed = (
        P(("dp", "tensor", "expert"), None),
        P(("dp", "tensor", "expert"), None),
        P(("dp", "tensor", "expert"), None),
        P(("dp", "tensor", "expert")),
        P("expert", None, ("dp", "tensor")),
        P("expert", None, ("dp", "tensor")),
        P("expert", ("dp", "tensor"), None),
    )
    return jax.shard_map(
        shards,
        mesh=mesh,
        in_specs=placed,
        out_specs=(P(("dp", "tensor", "expert"), None), P()),
        check_vma=False,
    )
```
